128 devices in a mesh: tok: 16 (over y_lo, x, core), tp: 8 (over z, y_hi).
Axes of the slice: x: 4, y: 4 (y_hi: 2, y_lo: 2; y = y_hi * 2 + y_lo), z: 4, core: 2. Of those that a mesh axis runs over, the one named last changes fastest.
Arguments:
- layer_input: bfloat16 [1536, 8192], P('tok'), may hold values from -45 to 45, as said below
- output_grad: bfloat16 [1536, 8192], P('tok'), may hold values from -45 to 45, as said below
- gate_weight: bfloat16 [8192, 16384], P('tok', 'tp'), may hold values from -0.0625 to 0.0625
- down_weight: bfloat16 [16384, 8192], P('tp', 'tok'), may hold values from -0.0625 to 0.0625
Outputs:
- input_gram: float32 [8192, 8192], P('tok', 'tp')
- grad_gram: float32 [16384, 16384], P('tp', 'tok')
The draws below stay inside these ranges and needn't reach their ends.
Inputs may be any that keep to these rules, and one draw needn't show every extreme that they name: `layer_input`: token rows and feature columns carry scales of their own. `output_grad`: token rows and feature columns carry scales of their own.
All inputs are finite; a program needn't handle non-finite values.
Results may differ from the reference program's by a relative error of at most 0.0039.
Values may be sent and summed in bfloat16 or wider, within the bound.
No kernel may reach another device: no remote copies, remote signals or barrier semaphores. Data moves between devices by JAX's collectives and lax.ppermute only.
A program may use at most 128 MiB of HBM per device.

```python
import math
import jax
import jax.numpy as jnp
from jax import lax

D = 8192
WFF = 16384
TOKENS = 1536


def token_scale(key):
    return jnp.exp(jax.random.uniform(key, (TOKENS, 1), jnp.float32, math.log(0.3), math.log(3.0)))


def scaled_field(key, base, row_scale):
    col_scale = jnp.exp(jax.random.uniform(key, (1, D), jnp.float32, math.log(0.3), math.log(3.0)))
    return (base * row_scale * col_scale).astype(jnp.bfloat16)


def draw_layer_input(key, part):
    row_scale = token_scale(key)
    key = jax.random.fold_in(key, 11)
    key_base = jax.random.fold_in(key, 0)
    key_scale = jax.random.fold_in(key, 2)
    base = jnp.clip(jax.random.normal(key_base, (TOKENS, D), jnp.float32), -5.0, 5.0)
    return scaled_field(key_scale, base, row_scale)


def draw_output_grad(key, part):
    row_scale = token_scale(key)
    key = jax.random.fold_in(key, 23)
    key_base = jax.random.fold_in(key, 0)
    key_scale = jax.random.fold_in(key, 2)
    key_energy = jax.random.fold_in(key, 3)
    energy = jnp.exp(jax.random.uniform(key_energy, (TOKENS, 1), jnp.float32, math.log(0.7), math.log(0.9)))
    base = jnp.clip(jax.random.normal(key_base, (TOKENS, D), jnp.float32), -5.0, 5.0)
    return scaled_field(key_scale, base, energy / row_scale)


def block_scale(key, shape, cuts, low, largest):
    level, own = 1.0, jax.random.fold_in(key, 6)
    for position, shards_of in cuts:
        steps = jnp.exp(jax.random.uniform(jax.random.fold_in(own, position), (shards_of,), jnp.float32, low / len(cuts), largest / len(cuts)))
        level = level * jnp.repeat(steps, shape[position] // shards_of).reshape([-1 if axis == position else 1 for axis in range(len(shape))])
    return level


def noise(stream_key, extent, width, most, cuts=(), dtype=jnp.bfloat16):
    array = width * jax.random.normal(stream_key, extent, jnp.float32)
    if cuts:
        array = array * block_scale(stream_key, extent, cuts, -0.22, 0.18)
    return jnp.clip(array, -most, most).astype(dtype)


def setup_inputs(seed: int = 0) -> dict:
    seeds = jax.random.split(jax.random.key(seed), 5)
    return {
        "layer_input": draw_layer_input(jax.random.fold_in(seeds[4], 71), 0),
        "output_grad": draw_output_grad(jax.random.fold_in(seeds[4], 71), 0),
        "gate_weight": noise(seeds[2], (D, WFF), D ** -0.5, 0.0625, ((0, 16), (1, 8))),
        "down_weight": noise(seeds[3], (WFF, D), D ** -0.5, 0.0625, ((0, 8), (1, 16))),
    }


def reference(layer_input, output_grad, gate_weight, down_weight):
    gate = jnp.dot(layer_input, gate_weight, preferred_element_type=jnp.float32)
    hidden_grad = lax.dot_general(output_grad, down_weight, (((1,), (1,)), ((), ())), preferred_element_type=jnp.float32)
    up_grad = (hidden_grad * jax.nn.silu(gate)).astype(jnp.bfloat16)
    input_gram = lax.dot_general(layer_input, layer_input, (((0,), (0,)), ((), ())), preferred_element_type=jnp.float32) / TOKENS
    grad_gram = lax.dot_general(up_grad, up_grad, (((0,), (0,)), ((), ())), preferred_element_type=jnp.float32) / TOKENS
    return input_gram, grad_gram
```

```python
import jax
import jax.numpy as jnp
from jax import lax
from jax.sharding import PartitionSpec as P

AXES = ("tok", "tp")
CHIPS = 8
CORES = 2
TOP = 32768.0
TINY = 1e-18


def contract_rows(left, right):
    return lax.dot_general(
        left, right, (((0,), (0,)), ((), ())), preferred_element_type=jnp.float32
    )


def contract_cols(left, right):
    return lax.dot_general(
        left, right, (((1,), (1,)), ((), ())), preferred_element_type=jnp.float32
    )


def routes(move):
    pairs = []
    for s in range(CHIPS):
        for c in range(CORES):
            for p in range(CHIPS):
                ns, nc, np_ = move(s, c, p)
                pairs.append(((s * CORES + c) * CHIPS + p, (ns * CORES + nc) * CHIPS + np_))
    return pairs


def send(value, move):
    return lax.ppermute(value, AXES, routes(move))


def swap_cores(value):
    return send(value, lambda s, c, p: (s, 1 - c, p))


SAME_CORE = [[s * CORES + c for s in range(CHIPS)] for c in range(CORES)]


def exchange(value, split_axis):
    return lax.all_to_all(
        value, "tok", split_axis, 0, axis_index_groups=SAME_CORE, tiled=True
    )


def in_core_order(core, own, other, axis):
    first = jnp.where(core == 0, own, other)
    second = jnp.where(core == 0, other, own)
    return jnp.concatenate([first, second], axis)


def largest(value, axis=None):
    return jnp.maximum(jnp.max(jnp.abs(value), axis=axis).astype(jnp.float32), TINY)


def reduce_partials(partial, row_top, weight_top, own_tops):
    depth = 1024.0
    scaled = (partial * (TOP / depth / (row_top[:, None] * weight_top))).astype(jnp.float16)
    parts = exchange(scaled, 0).reshape(CHIPS, -1, partial.shape[1])
    back = own_tops.T[:, :, None] * (weight_top * (depth / TOP))
    return jnp.sum(parts.astype(jnp.float32) * back, axis=0)


def shards(layer_input, output_grad, gate_weight, down_weight):
    rows = layer_input.shape[0]
    total = rows * CHIPS * CORES
    place = lax.axis_index("tok")
    chip, core = place // CORES, place % CORES
    band = lax.axis_index("tp")
    width = layer_input.shape[1] // CHIPS

    other_gate = swap_cores(gate_weight)
    other_down = swap_cores(down_weight)
    gate_full = in_core_order(core, gate_weight, other_gate, 0)
    down_full = in_core_order(core, down_weight, other_down, 1)
    tops = jnp.stack([largest(gate_full), largest(down_full)])
    for bit in (1, 2, 4):
        tops = jnp.maximum(tops, send(tops, lambda s, c, p: (s ^ bit, c, p)))
    own_input_tops = largest(layer_input.reshape(rows, CHIPS, width), 2)
    own_grad_tops = largest(output_grad.reshape(rows, CHIPS, width), 2)

    input_cols = exchange(layer_input, 1)
    gate = reduce_partials(
        jnp.dot(input_cols, gate_full, preferred_element_type=jnp.float32),
        largest(input_cols, 1),
        tops[0],
        own_input_tops,
    )
    grad_cols = exchange(output_grad, 1)
    hidden_grad = reduce_partials(
        contract_cols(grad_cols, down_full),
        largest(grad_cols, 1),
        tops[1],
        own_grad_tops,
    )

    own_band = lax.dynamic_slice_in_dim(layer_input, band * width, width, 1)
    band_rows = lax.all_gather(own_band, "tok", axis=0, tiled=True)
    half = width // CORES
    mine = lax.dynamic_slice_in_dim(input_cols, core * half, half, 1)
    theirs = swap_cores(lax.dynamic_slice_in_dim(input_cols, (1 - core) * half, half, 1))
    left = in_core_order(
        core, mine.reshape(CHIPS, 1, rows, half), theirs.reshape(CHIPS, 1, rows, half), 1
    ).reshape(total, half)
    input_gram = contract_rows(left, band_rows) / total

    up_grad = (hidden_grad * (gate / (1.0 + jnp.exp(-gate)))).astype(jnp.bfloat16)
    all_rows = lax.all_gather(up_grad, "tok", axis=0, tiled=True)
    moved = send(up_grad, lambda s, c, p: (s, c, s ^ p))
    moved = send(moved, lambda s, c, p: (s ^ p, c, p))
    units = up_grad.shape[1]
    gathered = jnp.zeros((CHIPS, rows, units), jnp.bfloat16)
    for k in range(CHIPS):
        piece = moved if k == 0 else send(moved, lambda s, c, p: (s, c, p ^ k))
        gathered = lax.dynamic_update_slice(
            gathered, piece[None], (jnp.bitwise_xor(jnp.bitwise_xor(band, chip), k), 0, 0)
        )
    half = units // CORES
    mine = lax.dynamic_slice_in_dim(gathered, core * half, half, 2)
    theirs = swap_cores(lax.dynamic_slice_in_dim(gathered, (1 - core) * half, half, 2))
    cols = in_core_order(core, mine[:, None], theirs[:, None], 1).reshape(total, half)
    grad_gram = contract_rows(all_rows, cols) / total
    return (input_gram, grad_gram)


def solution(mesh):
    placed = (P("tok", None), P("tok", None), P("tok", "tp"), P("tp", "tok"))
    return jax.shard_map(
        shards,
        mesh=mesh,
        in_specs=placed,
        out_specs=(P("tok", "tp"), P("tp", "tok")),
        check_vma=False,
    )
```

```python
import functools

import jax
import jax.numpy as jnp
from jax import lax
from jax.experimental import pallas as pl
from jax.experimental.pallas import tpu as pltpu
from jax.sharding import PartitionSpec as P

AXES = ("tok", "tp")
YL, X, CORE, Z, YH = 2, 4, 2, 4, 2
LANES = 128
LN2 = 0.6931471805599453
TINY = 1e-30


def contract_rows(left, right):
    return lax.dot_general(
        left, right, (((0,), (0,)), ((), ())), preferred_element_type=jnp.float32
    )


def contract_cols(left, right):
    return lax.dot_general(
        left, right, (((1,), (1,)), ((), ())), preferred_element_type=jnp.float32
    )


def index_of(yl, x, c, z, yh):
    return ((yl * X + x) * CORE + c) * (Z * YH) + z * YH + yh


def send(value, move):
    pairs = [
        (index_of(yl, x, c, z, yh), index_of(*move(yl, x, c, z, yh)))
        for yl in range(YL)
        for x in range(X)
        for c in range(CORE)
        for z in range(Z)
        for yh in range(YH)
    ]
    return lax.ppermute(value, AXES, pairs)


def over_core(value):
    return send(value, lambda yl, x, c, z, yh: (yl, x, 1 - c, z, yh))


def over_yl(value):
    return send(value, lambda yl, x, c, z, yh: (1 - yl, x, c, z, yh))


def over_other_y(value):
    return send(value, lambda yl, x, c, z, yh: (1 - yl, x, c, z, 1 - yh))


def over_yh(value):
    return send(value, lambda yl, x, c, z, yh: (yl, x, c, z, 1 - yh))


def over_x(value, k):
    return send(value, lambda yl, x, c, z, yh: (yl, x ^ k, c, z, yh))


def over_z(value, k):
    return send(value, lambda yl, x, c, z, yh: (yl, x, c, z ^ k, yh))


def turn_tp(yl, x, c, z, yh):
    p = (z * YH + yh) ^ (c * X + x)
    return yl, x, c, p // YH, p % YH


def turn_tok(yl, x, c, z, yh):
    s = (z * YH + yh) ^ (c * X + x)
    return s // X, s % X, yl, z, yh


def part(value, index, count, axis):
    size = value.shape[axis] // count
    return lax.dynamic_slice_in_dim(value, index * size, size, axis)


def after(value, *others):
    return lax.optimization_barrier((value, *others))[0]


def scaled_kernel(contract, count, *refs):
    fields, weights, out_ref = refs[:count], refs[count:-1], refs[-1]
    size = weights[0].shape[1 if contract else 0]
    units = out_ref.shape[1] - LANES
    tile = 256
    blocks = [(field, i * size) for field in fields for i in range(field.shape[1] // size)]

    def step(n, top):
        columns = pl.ds(pl.multiple_of(n * tile, tile), tile)
        total = None
        for (field, start), weight in zip(blocks, weights):
            block = weight[columns, :] if contract else weight[:, columns]
            term = lax.dot_general(
                field[:, start : start + size],
                block,
                (((1,), (1 if contract else 0,)), ((), ())),
                preferred_element_type=jnp.float32,
            )
            total = term if total is None else total + term
        out_ref[:, columns] = total
        for i in range(tile // LANES):
            top = jnp.maximum(top, jnp.abs(total[:, i * LANES : (i + 1) * LANES]))
        return top

    top = lax.fori_loop(
        0, units // tile, step, jnp.zeros((out_ref.shape[0], LANES), jnp.float32)
    )
    top = jnp.maximum(jnp.max(top, axis=1, keepdims=True), TINY)
    exponent = jnp.floor(14.0 - jnp.log(top) / LN2)
    out_ref[:, :units] *= jnp.exp(exponent * LN2)
    out_ref[:, units:] = jnp.broadcast_to(exponent, (out_ref.shape[0], LANES))


def scaled_product(fields, weights, contract):
    units = weights[0].shape[0 if contract else 1]
    rows = fields[0].shape[0]
    depth = sum(weight.shape[1 if contract else 0] for weight in weights)
    vmem = pl.BlockSpec(memory_space=pltpu.VMEM)
    return pl.pallas_call(
        functools.partial(scaled_kernel, contract, len(fields)),
        out_shape=jax.ShapeDtypeStruct((rows, units + LANES), jnp.float32),
        in_specs=[vmem] * (len(fields) + len(weights)),
        out_specs=vmem,
        compiler_params=pltpu.CompilerParams(vmem_limit_bytes=32 * 2**20),
        cost_estimate=pl.CostEstimate(
            flops=2 * rows * depth * units,
            bytes_accessed=2 * depth * (rows + units) + 4 * rows * units,
            transcendentals=0,
        ),
        name="scaled_product",
    )(*fields, *weights)


def gram_kernel(scale, places, left00, left01, left10, left11, *refs):
    pieces, out_ref, right, sems = refs[:-3], refs[-3], refs[-2], refs[-1]
    b = pl.program_id(0)

    @pl.when((b == 0) & (pl.program_id(1) == 0))
    def _():
        copies = []
        for i, piece in enumerate(pieces):
            for j in range(YH):
                slot = i * YH + j
                copies.append(
                    pltpu.make_async_copy(piece.at[j], right.at[places[slot]], sems.at[slot])
                )
        for copy in copies:
            copy.start()
        for copy in copies:
            copy.wait()

    def tokens(left):
        block = left[...]
        return block.reshape(block.shape[0] * block.shape[2], block.shape[3])

    for which, order in ((0, (left00, left01, left10, left11)), (1, (left10, left11, left00, left01))):

        @pl.when(b == which)
        def _():
            block = jnp.concatenate([tokens(left) for left in order], 0)
            rows = right[...]
            rows = rows.reshape(rows.shape[0] * rows.shape[1], rows.shape[2])
            out_ref[...] = contract_rows(block, rows) * scale


def grad_gram_of(lefts, pieces, places, yl, total):
    _, _, rows, units = lefts[0].shape
    tile = 256
    tiles = units // tile
    block = pl.BlockSpec((X, 1, rows, tile), lambda b, n, *_: (0, b, 0, n))
    slots = YL * CORE * X
    return pl.pallas_call(
        functools.partial(gram_kernel, 1.0 / total),
        out_shape=jax.ShapeDtypeStruct((YL * units, units), jnp.float32),
        grid_spec=pltpu.PrefetchScalarGridSpec(
            num_scalar_prefetch=1,
            grid=(YL, tiles),
            in_specs=[block] * 4 + [pl.BlockSpec(memory_space=pl.ANY)] * len(pieces),
            out_specs=pl.BlockSpec(
                (tile, units), lambda b, n, places: ((places[slots] ^ b) * tiles + n, 0)
            ),
            scratch_shapes=[
                pltpu.VMEM((slots, rows, units), jnp.bfloat16),
                pltpu.SemaphoreType.DMA((slots,)),
            ],
        ),
        compiler_params=pltpu.CompilerParams(vmem_limit_bytes=40 * 2**20),
        cost_estimate=pl.CostEstimate(
            flops=2 * total * YL * units * units,
            bytes_accessed=6 * total * units + 8 * units * units,
            transcendentals=0,
        ),
        name="grad_gram",
    )(places, *lefts, *pieces)


def shards(layer_input, output_grad, gate_weight, down_weight):
    rows, model = layer_input.shape
    total = rows * YL * X * CORE
    place, band = lax.axis_index("tok"), lax.axis_index("tp")
    chip, c = place // CORE, place % CORE
    yl, x = chip // X, chip % X
    width = model // (YL * X)
    half = width // CORE

    def cut(field, *more):
        return [
            jnp.concatenate(
                [
                    part(field, (((yl ^ b) * X + (x ^ k)) * CORE + (c ^ d)), YL * X * CORE, 1)
                    for d in range(CORE)
                    for b in range(YL)
                ]
                + list(more),
                1,
            )
            for k in range(X)
        ]

    def swapped(pieces):
        return [pieces[1], pieces[0], pieces[3], pieces[2]]

    def halved(parts):
        parts = [part.astype(jnp.float16).reshape(X, rows, -1) for part in parts]
        return jnp.concatenate(parts, 2) if len(parts) > 1 else parts[0]

    def exchanged(parts):
        return [parts[0]] + [over_x(parts[k], k) for k in range(1, X)]

    def summed(pieces):
        total_sum = None
        for piece in pieces:
            piece = piece.astype(jnp.float32)
            term = piece[:, :-LANES] * jnp.exp(piece[:, -LANES : 1 - LANES] * -LN2)
            total_sum = term if total_sum is None else total_sum + term
        return total_sum

    def activated(gate, hidden):
        return (hidden * (gate / (1.0 + jnp.exp(-gate)))).astype(jnp.bfloat16)

    def round_x(both):
        return jnp.stack([both if k == 0 else over_x(both, k) for k in range(X)])

    gate_near = part(gate_weight, yl, YL, 1)
    gate_across = over_yl(part(gate_weight, 1 - yl, YL, 1))
    input_cut = cut(layer_input)
    input_first = over_other_y(input_cut[0])
    pieces = [over_x(input_cut[k], k) for k in range(1, X)]
    own_band = part(layer_input, band, YL * X, 1)
    grad_cut = cut(output_grad, own_band)
    gate_across, input_first, pieces, grad_cut = lax.optimization_barrier(
        (gate_across, input_first, pieces, grad_cut)
    )
    gate_other = over_core(jnp.stack([gate_near, gate_across]))
    input_rest = over_other_y(jnp.concatenate(pieces, 0))
    input_own = jnp.concatenate([input_cut[0]] + pieces, 0)
    grad_pieces = [over_x(grad_cut[k], k) for k in range(1, X)]

    gate_pieces = [gate_near, gate_across, gate_other[0], gate_other[1]]
    gate_part = halved([scaled_product([input_own], gate_pieces, False)])
    down_near = part(down_weight, yl, YL, 0)
    down_across = over_yl(after(part(down_weight, 1 - yl, YL, 0), gate_other))
    grad_pieces, input_first, input_rest = after(
        (grad_pieces, input_first, input_rest), gate_part
    )
    gate_sent = exchanged(after(gate_part, *grad_pieces))
    grad_both = jnp.concatenate([grad_cut[0]] + grad_pieces, 0)
    split = 3 * half
    near = over_yl(after(grad_both[:, split:], gate_part))
    far = over_other_y(after(grad_both[:, :split], input_rest))
    input_other = jnp.concatenate([input_first, input_rest], 0)
    gate_part = scaled_product([input_other], swapped(gate_pieces), False)

    down_across = after(down_across, gate_part)
    down_other = over_core(jnp.stack([down_near, down_across]))
    down_pieces = [down_near, down_across, down_other[0], down_other[1]]
    gate = summed(after(gate_sent, gate_part))
    hidden_part = scaled_product([after(grad_both, gate)], down_pieces, True)
    mixed_sent = exchanged(halved([hidden_part, gate_part]))
    near, far = after([near, far], hidden_part)
    hidden_part = halved([scaled_product([far, near], swapped(down_pieces), True)])
    hidden_sent = exchanged(hidden_part)
    mixed_sent = after(mixed_sent, hidden_part)
    cuts = mixed_sent[0].shape[1] // 2
    first = activated(gate, summed([piece[:, :cuts] for piece in mixed_sent]))
    gate = summed([piece[:, cuts:] for piece in mixed_sent])
    moved = send(first, turn_tp)
    both = jnp.stack([first, over_yl(first)])
    moved, both, hidden_sent = lax.optimization_barrier((moved, both, hidden_sent))
    first_round = round_x(both)
    second = activated(gate, summed(hidden_sent))
    moved = send(moved, turn_tok)
    pair = jnp.stack([moved, over_yh(moved)])
    first_turned = [pair] + [over_z(pair, k) for k in range(1, Z)]
    both = jnp.stack([second, over_yl(second)])
    moved = send(send(second, turn_tp), turn_tok)
    pair = jnp.stack([moved, over_yh(moved)])
    second_turned = [pair] + [over_z(pair, k) for k in range(1, Z)]
    second_round = round_x(after(both, *first_turned))
    first_gathered = [first_round, over_core(after(first_round, pair))]
    second_gathered = [second_round, over_core(second_round)]

    bands = jnp.stack([grad_both[:, YL * width :], near[:, half:]])
    mine = jnp.stack([input_own[:, :half], input_other[:, half : 2 * half]])
    theirs = jnp.stack([input_own[:, 2 * half : 3 * half], input_other[:, 3 * half :]])
    across = over_core(after(jnp.concatenate([theirs, bands], 2), first))
    left = jnp.stack([mine, across[:, :, :half]]).reshape(total, half)
    right = jnp.stack([bands, across[:, :, half:]]).reshape(total, width)
    input_gram = contract_rows(left, right) / total

    turn = band ^ chip ^ (c * X + x)
    places = [
        (yl ^ c ^ h) * (CORE * X) + (turn ^ j) for h in range(YL) for j in range(Z * YH)
    ]
    grad_gram = grad_gram_of(
        first_gathered + second_gathered,
        first_turned + after(second_turned, input_gram),
        jnp.stack(places + [yl]).astype(jnp.int32),
        yl,
        total,
    )

    return (input_gram, grad_gram)


def solution(mesh):
    placed = (P("tok", None), P("tok", None), P("tok", "tp"), P("tp", "tok"))
    return jax.shard_map(
        shards,
        mesh=mesh,
        in_specs=placed,
        out_specs=(P("tok", "tp"), P("tp", "tok")),
        check_vma=False,
    )
```

```python
import functools

import jax
import jax.numpy as jnp
from jax import lax
from jax.experimental import pallas as pl
from jax.experimental.pallas import tpu as pltpu
from jax.sharding import PartitionSpec as P

AXES = ("tok", "tp")
YL, X, CORE, Z, YH = 2, 4, 2, 4, 2
LANES = 128
LN2 = 0.6931471805599453
TINY = 1e-30


def contract_rows(left, right):
    return lax.dot_general(
        left, right, (((0,), (0,)), ((), ())), preferred_element_type=jnp.float32
    )


def contract_cols(left, right):
    return lax.dot_general(
        left, right, (((1,), (1,)), ((), ())), preferred_element_type=jnp.float32
    )


def index_of(yl, x, c, z, yh):
    return ((yl * X + x) * CORE + c) * (Z * YH) + z * YH + yh


def send(value, move):
    pairs = [
        (index_of(yl, x, c, z, yh), index_of(*move(yl, x, c, z, yh)))
        for yl in range(YL)
        for x in range(X)
        for c in range(CORE)
        for z in range(Z)
        for yh in range(YH)
    ]
    return lax.ppermute(value, AXES, pairs)


def over_core(value):
    return send(value, lambda yl, x, c, z, yh: (yl, x, 1 - c, z, yh))


def over_yl(value):
    return send(value, lambda yl, x, c, z, yh: (1 - yl, x, c, z, yh))


def over_other_y(value):
    return send(value, lambda yl, x, c, z, yh: (1 - yl, x, c, z, 1 - yh))


def over_yh(value):
    return send(value, lambda yl, x, c, z, yh: (yl, x, c, z, 1 - yh))


def over_x(value, k):
    return send(value, lambda yl, x, c, z, yh: (yl, x ^ k, c, z, yh))


def over_z(value, k):
    return send(value, lambda yl, x, c, z, yh: (yl, x, c, z ^ k, yh))


def turn_tp(yl, x, c, z, yh):
    p = (z * YH + yh) ^ (c * X + x)
    return yl, x, c, p // YH, p % YH


def turn_tok(yl, x, c, z, yh):
    s = (z * YH + yh) ^ (c * X + x)
    return s // X, s % X, yl, z, yh


def turn_tok_yh(yl, x, c, z, yh):
    yl, x, c, z, yh = turn_tok(yl, x, c, z, yh)
    return yl, x, c, z, 1 - yh


def part(value, index, count, axis):
    size = value.shape[axis] // count
    return lax.dynamic_slice_in_dim(value, index * size, size, axis)


def after(value, *others):
    return lax.optimization_barrier((value, *others))[0]


def scaled_kernel(contract, count, *refs):
    fields, weights, out_ref = refs[:count], refs[count:-1], refs[-1]
    size = weights[0].shape[1 if contract else 0]
    units = out_ref.shape[1] - LANES
    tile = 256
    blocks = [(field, i * size) for field in fields for i in range(field.shape[1] // size)]

    def step(n, top):
        columns = pl.ds(pl.multiple_of(n * tile, tile), tile)
        total = None
        for (field, start), weight in zip(blocks, weights):
            block = weight[columns, :] if contract else weight[:, columns]
            term = lax.dot_general(
                field[:, start : start + size],
                block,
                (((1,), (1 if contract else 0,)), ((), ())),
                preferred_element_type=jnp.float32,
            )
            total = term if total is None else total + term
        out_ref[:, columns] = total
        for i in range(tile // LANES):
            top = jnp.maximum(top, jnp.abs(total[:, i * LANES : (i + 1) * LANES]))
        return top

    top = lax.fori_loop(
        0, units // tile, step, jnp.zeros((out_ref.shape[0], LANES), jnp.float32)
    )
    top = jnp.maximum(jnp.max(top, axis=1, keepdims=True), TINY)
    exponent = jnp.floor(14.0 - jnp.log(top) / LN2)
    out_ref[:, :units] *= jnp.exp(exponent * LN2)
    out_ref[:, units:] = jnp.broadcast_to(exponent, (out_ref.shape[0], LANES))


def scaled_product(fields, weights, contract):
    units = weights[0].shape[0 if contract else 1]
    rows = fields[0].shape[0]
    depth = sum(weight.shape[1 if contract else 0] for weight in weights)
    vmem = pl.BlockSpec(memory_space=pltpu.VMEM)
    return pl.pallas_call(
        functools.partial(scaled_kernel, contract, len(fields)),
        out_shape=jax.ShapeDtypeStruct((rows, units + LANES), jnp.float32),
        in_specs=[vmem] * (len(fields) + len(weights)),
        out_specs=vmem,
        compiler_params=pltpu.CompilerParams(vmem_limit_bytes=16 * 2**20),
        cost_estimate=pl.CostEstimate(
            flops=2 * rows * depth * units,
            bytes_accessed=2 * depth * (rows + units) + 4 * rows * units,
            transcendentals=0,
        ),
        name="scaled_product",
    )(*fields, *weights)


def gram_kernel(scale, lefts, places, *refs):
    lefts, pieces = refs[:lefts], refs[lefts:-3]
    out_ref, right, sems = refs[-3:]
    b = pl.program_id(0)

    @pl.when((b == 0) & (pl.program_id(1) == 0))
    def _():
        copies = []
        tiles = [piece.at[j] for piece in pieces for j in range(piece.shape[0])]
        for i, tile in enumerate(tiles):
            for h in range(YL):
                slot = h * len(tiles) + i
                copies.append(
                    pltpu.make_async_copy(tile.at[h], right.at[places[slot]], sems.at[slot])
                )
        for copy in copies:
            copy.start()
        for copy in copies:
            copy.wait()

    def tokens(left, h):
        block = left[:, 0, h]
        return block.reshape(block.shape[0] * block.shape[1], block.shape[2])

    for which in range(YL):

        @pl.when(b == which)
        def _():
            block = jnp.concatenate(
                [tokens(left, h ^ which) for h in range(YL) for left in lefts], 0
            )
            rows = right[...]
            rows = rows.reshape(rows.shape[0] * rows.shape[1], rows.shape[2])
            out_ref[...] = contract_rows(block, rows) * scale


def grad_gram_of(lefts, pieces, places, yl, total):
    rows, units = lefts[0].shape[3:]
    tile = 512
    tiles = units // tile
    slots = YL * CORE * X
    return pl.pallas_call(
        functools.partial(gram_kernel, 1.0 / total, len(lefts)),
        out_shape=jax.ShapeDtypeStruct((YL * units, units), jnp.float32),
        grid_spec=pltpu.PrefetchScalarGridSpec(
            num_scalar_prefetch=1,
            grid=(YL, tiles),
            in_specs=[
                pl.BlockSpec(
                    (left.shape[0], 1, YL, rows, tile), lambda b, n, *_: (0, b, 0, 0, n)
                )
                for left in lefts
            ]
            + [pl.BlockSpec(memory_space=pltpu.HBM)] * len(pieces),
            out_specs=pl.BlockSpec(
                (tile, units), lambda b, n, places: ((places[slots] ^ b) * tiles + n, 0)
            ),
            scratch_shapes=[
                pltpu.VMEM((slots, rows, units), jnp.bfloat16),
                pltpu.SemaphoreType.DMA((slots,)),
            ],
        ),
        compiler_params=pltpu.CompilerParams(vmem_limit_bytes=24 * 2**20),
        cost_estimate=pl.CostEstimate(
            flops=2 * total * YL * units * units,
            bytes_accessed=6 * total * units + 8 * units * units,
            transcendentals=0,
        ),
        name="grad_gram",
    )(places, *lefts, *pieces)


def shards(layer_input, output_grad, gate_weight, down_weight):
    rows, model = layer_input.shape
    total = rows * YL * X * CORE
    place, band = lax.axis_index("tok"), lax.axis_index("tp")
    chip, c = place // CORE, place % CORE
    yl, x = chip // X, chip % X
    width = model // (YL * X)
    half = width // CORE

    def cut(field, *more):
        return [
            jnp.concatenate(
                [
                    part(field, (((yl ^ b) * X + (x ^ k)) * CORE + (c ^ d)), YL * X * CORE, 1)
                    for d in range(CORE)
                    for b in range(YL)
                ]
                + list(more),
                1,
            )
            for k in range(X)
        ]

    def swapped(pieces):
        return [pieces[1], pieces[0], pieces[3], pieces[2]]

    def halved(parts):
        parts = [part.astype(jnp.float16).reshape(X, rows, -1) for part in parts]
        return jnp.concatenate(parts, 2) if len(parts) > 1 else parts[0]

    def exchanged(parts):
        return [parts[0]] + [over_x(parts[k], k) for k in range(1, X)]

    def summed(pieces):
        total_sum = None
        for piece in pieces:
            piece = piece.astype(jnp.float32)
            term = piece[:, :-LANES] * jnp.exp(piece[:, -LANES : 1 - LANES] * -LN2)
            total_sum = term if total_sum is None else total_sum + term
        return total_sum

    def activated(gate, hidden):
        return (hidden * (gate / (1.0 + jnp.exp(-gate)))).astype(jnp.bfloat16)

    gate_near = part(gate_weight, yl, YL, 1)
    gate_far = part(gate_weight, 1 - yl, YL, 1)
    gate_across = over_yl(gate_far)
    input_cut = cut(after(layer_input, gate_far))
    input_first = over_other_y(input_cut[0])
    pieces = [over_x(input_cut[k], k) for k in range(1, X)]
    own_band = part(layer_input, band, YL * X, 1)
    grad_cut = cut(output_grad, own_band)
    down_near, down_far = part(down_weight, yl, YL, 0), part(down_weight, 1 - yl, YL, 0)
    gate_across, input_first, pieces, grad_cut, down_far = lax.optimization_barrier(
        (gate_across, input_first, pieces, grad_cut, down_far)
    )
    gate_other = over_core(jnp.stack([gate_near, gate_across]))
    input_rest = over_other_y(jnp.concatenate(pieces, 0))
    down_across = over_yl(down_far)
    input_own = jnp.concatenate([input_cut[0]] + pieces, 0)
    grad_pieces = [over_x(grad_cut[k], k) for k in range(1, X)]

    gate_pieces = [gate_near, gate_across, gate_other[0], gate_other[1]]
    gate_part = scaled_product([input_own], gate_pieces, False)
    grad_pieces, down_across, input_rest, gate_part = lax.optimization_barrier(
        (grad_pieces, down_across, input_rest, gate_part)
    )
    down_other = over_core(jnp.stack([down_near, down_across]))
    down_pieces = [down_near, down_across, down_other[0], down_other[1]]
    grad_both = jnp.concatenate([grad_cut[0]] + grad_pieces, 0)
    far, near, band_own = jnp.split(grad_both, [width, 2 * width], 1)
    near, far, band_own, grad_both = lax.optimization_barrier((near, far, band_own, grad_both))
    near = over_yl(near)
    far = over_other_y(far)
    hidden_part = scaled_product([grad_both], down_pieces, True)
    first_sent = exchanged(halved([gate_part, hidden_part]))
    input_other = jnp.concatenate([input_first, input_rest], 0)
    gate_part = scaled_product(
        [after(input_other, hidden_part)], swapped(gate_pieces), False
    )
    near, far = after([near, far], gate_part, first_sent[1], first_sent[3])
    hidden_part = scaled_product([far, near], swapped(down_pieces), True)
    second_sent = exchanged(halved([gate_part, hidden_part]))
    band_other = over_yl(after(band_own, near))
    second_sent, band_other = lax.optimization_barrier((second_sent, band_other))

    def up_grads(sent):
        cuts = sent[0].shape[1] // 2
        gate = summed([piece[:, :cuts] for piece in sent])
        return activated(gate, summed([piece[:, cuts:] for piece in sent]))

    first = up_grads(after(first_sent, hidden_part))
    up_grad = jnp.stack([first, up_grads(after(second_sent, first))])
    moved = send(up_grad, turn_tp)
    both = jnp.stack([up_grad, over_yl(up_grad)])
    pair = jnp.stack([send(moved, turn_tok), send(moved, turn_tok_yh)])
    pair, both = lax.optimization_barrier((pair, both))
    ring = [over_x(both, 1), over_x(both, 3), over_z(pair, 1), over_z(pair, 3)]
    ring, both, pair = lax.optimization_barrier((ring, both, pair))
    near_most = jnp.stack([both] + ring[:2])
    far_most = over_core(near_most)
    opposite = [
        over_x(ring[0][0], 3),
        over_x(ring[1][1], 1),
        over_z(ring[2][0], 3),
        over_z(ring[3][1], 1),
    ]
    bands = jnp.stack([band_own, band_other])
    mine = jnp.stack([input_own[:, :half], input_other[:, half : 2 * half]])
    theirs = jnp.stack([input_own[:, 2 * half : 3 * half], input_other[:, 3 * half :]])
    across = over_core(after(jnp.concatenate([theirs, bands], 2), pair))
    left = jnp.stack([mine, across[:, :, :half]]).reshape(total, half)
    right = jnp.stack([bands, across[:, :, half:]]).reshape(total, width)
    input_gram = contract_rows(left, right) / total

    opposite, input_gram = lax.optimization_barrier((opposite, input_gram))
    near_last = jnp.stack(opposite[:2])[None]
    turned = [pair, ring[2], opposite[2][None], opposite[3][None], ring[3]]
    rows_of = [near_most, near_last, far_most, over_core(near_last)]

    turn = band ^ chip ^ (c * X + x)
    places = []
    for h in range(YL):
        for j in range(Z * YH):
            tile = turn ^ j
            tile = tile ^ ((tile & (X - 1)) >> 1)
            places.append((yl ^ c ^ h) * (CORE * X) + tile)
    grad_gram = grad_gram_of(
        rows_of,
        turned,
        jnp.stack(places + [yl]).astype(jnp.int32),
        yl,
        total,
    )

    return (input_gram, grad_gram)


def solution(mesh):
    placed = (P("tok", None), P("tok", None), P("tok", "tp"), P("tp", "tok"))
    return jax.shard_map(
        shards,
        mesh=mesh,
        in_specs=placed,
        out_specs=(P("tok", "tp"), P("tp", "tok")),
        check_vma=False,
    )
```

```python
import functools

import jax
import jax.numpy as jnp
from jax import lax
from jax.experimental import pallas as pl
from jax.experimental.pallas import tpu as pltpu
from jax.sharding import PartitionSpec as P

AXES = ("tok", "tp")
YL, X, CORE, Z, YH = 2, 4, 2, 4, 2
LANES = 128
LN2 = 0.6931471805599453
TINY = 1e-30


def contract_rows(left, right):
    return lax.dot_general(
        left, right, (((0,), (0,)), ((), ())), preferred_element_type=jnp.float32
    )


def contract_cols(left, right):
    return lax.dot_general(
        left, right, (((1,), (1,)), ((), ())), preferred_element_type=jnp.float32
    )


def index_of(yl, x, c, z, yh):
    return ((yl * X + x) * CORE + c) * (Z * YH) + z * YH + yh


def send(value, move):
    pairs = [
        (index_of(yl, x, c, z, yh), index_of(*move(yl, x, c, z, yh)))
        for yl in range(YL)
        for x in range(X)
        for c in range(CORE)
        for z in range(Z)
        for yh in range(YH)
    ]
    return lax.ppermute(value, AXES, pairs)


def over_core(value):
    return send(value, lambda yl, x, c, z, yh: (yl, x, 1 - c, z, yh))


def over_yl(value):
    return send(value, lambda yl, x, c, z, yh: (1 - yl, x, c, z, yh))


def over_other_y(value):
    return send(value, lambda yl, x, c, z, yh: (1 - yl, x, c, z, 1 - yh))


def over_yh(value):
    return send(value, lambda yl, x, c, z, yh: (yl, x, c, z, 1 - yh))


def over_x(value, k):
    return send(value, lambda yl, x, c, z, yh: (yl, x ^ k, c, z, yh))


def over_z(value, k):
    return send(value, lambda yl, x, c, z, yh: (yl, x, c, z ^ k, yh))


def turn_tp(yl, x, c, z, yh):
    p = (z * YH + yh) ^ (c * X + x)
    return yl, x, c, p // YH, p % YH


def turn_tok(yl, x, c, z, yh):
    s = (z * YH + yh) ^ (c * X + x)
    return s // X, s % X, yl, z, yh


def turn_tok_yh(yl, x, c, z, yh):
    yl, x, c, z, yh = turn_tok(yl, x, c, z, yh)
    return yl, x, c, z, 1 - yh


def part(value, index, count, axis):
    size = value.shape[axis] // count
    return lax.dynamic_slice_in_dim(value, index * size, size, axis)


def after(value, *others):
    return lax.optimization_barrier((value, *others))[0]


def scaled_kernel(contract, count, *refs):
    fields, weights, out_ref = refs[:count], refs[count:-1], refs[-1]
    size = weights[0].shape[1 if contract else 0]
    units = out_ref.shape[1] - LANES
    tile = 256
    blocks = [(field, i * size) for field in fields for i in range(field.shape[1] // size)]

    def step(n, top):
        columns = pl.ds(pl.multiple_of(n * tile, tile), tile)
        total = None
        for (field, start), weight in zip(blocks, weights):
            block = weight[columns, :] if contract else weight[:, columns]
            term = lax.dot_general(
                field[:, start : start + size],
                block,
                (((1,), (1 if contract else 0,)), ((), ())),
                preferred_element_type=jnp.float32,
            )
            total = term if total is None else total + term
        out_ref[:, columns] = total
        for i in range(tile // LANES):
            top = jnp.maximum(top, jnp.abs(total[:, i * LANES : (i + 1) * LANES]))
        return top

    top = lax.fori_loop(
        0, units // tile, step, jnp.zeros((out_ref.shape[0], LANES), jnp.float32)
    )
    top = jnp.maximum(jnp.max(top, axis=1, keepdims=True), TINY)
    exponent = jnp.floor(14.0 - jnp.log(top) / LN2)
    out_ref[:, :units] *= jnp.exp(exponent * LN2)
    out_ref[:, units:] = jnp.broadcast_to(exponent, (out_ref.shape[0], LANES))


def scaled_product(fields, weights, contract):
    units = weights[0].shape[0 if contract else 1]
    rows = fields[0].shape[0]
    depth = sum(weight.shape[1 if contract else 0] for weight in weights)
    vmem = pl.BlockSpec(memory_space=pltpu.VMEM)
    return pl.pallas_call(
        functools.partial(scaled_kernel, contract, len(fields)),
        out_shape=jax.ShapeDtypeStruct((rows, units + LANES), jnp.float32),
        in_specs=[vmem] * (len(fields) + len(weights)),
        out_specs=vmem,
        compiler_params=pltpu.CompilerParams(vmem_limit_bytes=16 * 2**20),
        cost_estimate=pl.CostEstimate(
            flops=2 * rows * depth * units,
            bytes_accessed=2 * depth * (rows + units) + 4 * rows * units,
            transcendentals=0,
        ),
        name="scaled_product",
    )(*fields, *weights)


def product_kernel(scale, left_ref, right_ref, out_ref):
    out_ref[...] = contract_rows(left_ref[...], right_ref[...]) * scale


def input_gram_of(left, right):
    total, rows = left.shape
    width = right.shape[1]
    tile = 256
    return pl.pallas_call(
        functools.partial(product_kernel, 1.0 / total),
        out_shape=jax.ShapeDtypeStruct((rows, width), jnp.float32),
        grid=(rows // tile,),
        in_specs=[
            pl.BlockSpec((total, tile), lambda n: (0, n)),
            pl.BlockSpec((total, width), lambda n: (0, 0)),
        ],
        out_specs=pl.BlockSpec((tile, width), lambda n: (n, 0)),
        compiler_params=pltpu.CompilerParams(vmem_limit_bytes=20 * 2**20),
        cost_estimate=pl.CostEstimate(
            flops=2 * total * rows * width,
            bytes_accessed=2 * total * (rows + width) + 4 * rows * width,
            transcendentals=0,
        ),
        name="input_gram",
    )(left, right)


def gram_kernel(scale, lefts, places, *refs):
    lefts, pieces = refs[:lefts], refs[lefts:-3]
    out_ref, right, sems = refs[-3:]
    b = pl.program_id(0)

    @pl.when((b == 0) & (pl.program_id(1) == 0))
    def _():
        copies = []
        tiles = [piece.at[j] for piece in pieces for j in range(piece.shape[0])]
        for i, tile in enumerate(tiles):
            for h in range(YL):
                slot = h * len(tiles) + i
                copies.append(
                    pltpu.make_async_copy(tile.at[h], right.at[places[slot]], sems.at[slot])
                )
        for copy in copies:
            copy.start()
        for copy in copies:
            copy.wait()

    def tokens(left, h):
        block = left[:, 0, h]
        return block.reshape(block.shape[0] * block.shape[1], block.shape[2])

    for which in range(YL):

        @pl.when(b == which)
        def _():
            block = jnp.concatenate(
                [tokens(left, h ^ which) for h in range(YL) for left in lefts], 0
            )
            rows = right[...]
            rows = rows.reshape(rows.shape[0] * rows.shape[1], rows.shape[2])
            out_ref[...] = contract_rows(block, rows) * scale


def grad_gram_of(lefts, pieces, places, yl, total):
    rows, units = lefts[0].shape[3:]
    tile = 512
    tiles = units // tile
    slots = YL * CORE * X
    return pl.pallas_call(
        functools.partial(gram_kernel, 1.0 / total, len(lefts)),
        out_shape=jax.ShapeDtypeStruct((YL * units, units), jnp.float32),
        grid_spec=pltpu.PrefetchScalarGridSpec(
            num_scalar_prefetch=1,
            grid=(YL, tiles),
            in_specs=[
                pl.BlockSpec(
                    (left.shape[0], 1, YL, rows, tile), lambda b, n, *_: (0, b, 0, 0, n)
                )
                for left in lefts
            ]
            + [pl.BlockSpec(memory_space=pltpu.HBM)] * len(pieces),
            out_specs=pl.BlockSpec(
                (tile, units), lambda b, n, places: ((places[slots] ^ b) * tiles + n, 0)
            ),
            scratch_shapes=[
                pltpu.VMEM((slots, rows, units), jnp.bfloat16),
                pltpu.SemaphoreType.DMA((slots,)),
            ],
        ),
        compiler_params=pltpu.CompilerParams(vmem_limit_bytes=58 * 2**20),
        cost_estimate=pl.CostEstimate(
            flops=2 * total * YL * units * units,
            bytes_accessed=6 * total * units + 8 * units * units,
            transcendentals=0,
        ),
        name="grad_gram",
    )(places, *lefts, *pieces)


def shards(layer_input, output_grad, gate_weight, down_weight):
    rows, model = layer_input.shape
    total = rows * YL * X * CORE
    place, band = lax.axis_index("tok"), lax.axis_index("tp")
    chip, c = place // CORE, place % CORE
    yl, x = chip // X, chip % X
    width = model // (YL * X)
    half = width // CORE

    def cut(field, *more):
        return [
            jnp.concatenate(
                [
                    part(field, (((yl ^ b) * X + (x ^ k)) * CORE + (c ^ d)), YL * X * CORE, 1)
                    for d in range(CORE)
                    for b in range(YL)
                ]
                + list(more),
                1,
            )
            for k in range(X)
        ]

    def swapped(pieces):
        return [pieces[1], pieces[0], pieces[3], pieces[2]]

    def halved(parts):
        parts = [part.astype(jnp.float16).reshape(X, rows, -1) for part in parts]
        return jnp.concatenate(parts, 2) if len(parts) > 1 else parts[0]

    def exchanged(parts):
        return [parts[0]] + [over_x(parts[k], k) for k in range(1, X)]

    def summed(pieces):
        total_sum = None
        for piece in pieces:
            piece = piece.astype(jnp.float32)
            term = piece[:, :-LANES] * jnp.exp(piece[:, -LANES : 1 - LANES] * -LN2)
            total_sum = term if total_sum is None else total_sum + term
        return total_sum

    def activated(gate, hidden):
        return (hidden * (gate / (1.0 + jnp.exp(-gate)))).astype(jnp.bfloat16)

    input_cut = cut(layer_input)
    gate_weight = after(gate_weight, *input_cut)
    gate_near = part(gate_weight, yl, YL, 1)
    gate_far = part(gate_weight, 1 - yl, YL, 1)
    gate_across = over_yl(gate_far)
    input_first = over_other_y(input_cut[0])
    pieces = [over_x(input_cut[k], k) for k in range(1, X)]
    own_band = part(layer_input, band, YL * X, 1)
    grad_cut = cut(output_grad, own_band)
    down_near, down_far = part(down_weight, yl, YL, 0), part(down_weight, 1 - yl, YL, 0)
    gate_across, input_first, pieces, grad_cut, down_far = lax.optimization_barrier(
        (gate_across, input_first, pieces, grad_cut, down_far)
    )
    gate_other = over_core(jnp.stack([gate_near, gate_across]))
    input_rest = over_other_y(jnp.concatenate(pieces, 0))
    down_across = over_yl(down_far)
    input_own = jnp.concatenate([input_cut[0]] + pieces, 0)
    grad_pieces = [over_x(grad_cut[k], k) for k in range(1, X)]

    gate_pieces = [gate_near, gate_across, gate_other[0], gate_other[1]]
    gate_part = scaled_product([input_own], gate_pieces, False)
    grad_pieces, down_across, input_rest, gate_part = lax.optimization_barrier(
        (grad_pieces, down_across, input_rest, gate_part)
    )
    down_other = over_core(jnp.stack([down_near, down_across]))
    down_pieces = [down_near, down_across, down_other[0], down_other[1]]
    grad_both = jnp.concatenate([grad_cut[0]] + grad_pieces, 0)
    far, near, band_own = jnp.split(grad_both, [width, 2 * width], 1)
    near, far, band_own, grad_both = lax.optimization_barrier((near, far, band_own, grad_both))
    near = over_yl(near)
    far = over_other_y(far)
    hidden_part = scaled_product([grad_both], down_pieces, True)
    first_sent = exchanged(halved([gate_part, hidden_part]))
    input_other = jnp.concatenate([input_first, input_rest], 0)
    gate_part = scaled_product(
        [after(input_other, hidden_part)], swapped(gate_pieces), False
    )
    near, far = after([near, far], gate_part, first_sent[1], first_sent[3])
    hidden_part = scaled_product([far, near], swapped(down_pieces), True)
    second_sent = exchanged(halved([gate_part, hidden_part]))
    band_other = over_yl(after(band_own, near))
    second_sent, band_other = lax.optimization_barrier((second_sent, band_other))

    def up_grads(sent):
        cuts = sent[0].shape[1] // 2
        gate = summed([piece[:, :cuts] for piece in sent])
        return activated(gate, summed([piece[:, cuts:] for piece in sent]))

    first = up_grads(after(first_sent, hidden_part))
    up_grad = jnp.stack([first, up_grads(after(second_sent, first))])
    moved = send(up_grad, turn_tp)
    both = jnp.stack([up_grad, over_yl(up_grad)])
    pair = jnp.stack([send(moved, turn_tok), send(moved, turn_tok_yh)])
    bands = jnp.stack([band_own, band_other])
    mine = jnp.stack([input_own[:, :half], input_other[:, half : 2 * half]])
    theirs = jnp.stack([input_own[:, 2 * half : 3 * half], input_other[:, 3 * half :]])
    across = over_core(after(jnp.concatenate([theirs, bands], 2), moved))
    pair, both, across = lax.optimization_barrier((pair, both, across))
    left = jnp.stack([mine, across[:, :, :half]]).reshape(total, half)
    right = jnp.stack([bands, across[:, :, half:]]).reshape(total, width)
    input_gram = input_gram_of(left, right)

    ring = [over_x(both, 1), over_x(both, 3), over_z(pair, 1), over_z(pair, 3)]
    ring, both, pair, input_gram = lax.optimization_barrier((ring, both, pair, input_gram))
    near_most = jnp.stack([both] + ring[:2])
    far_most = over_core(near_most)
    opposite = [
        over_x(ring[0][0], 3),
        over_x(ring[1][1], 1),
        over_z(ring[2][0], 3),
        over_z(ring[3][1], 1),
    ]
    opposite = lax.optimization_barrier(opposite)
    near_last = jnp.stack(opposite[:2])[None]
    turned = [pair, ring[2], opposite[2][None], opposite[3][None], ring[3]]
    rows_of = [near_most, near_last, far_most, over_core(near_last)]

    turn = band ^ chip ^ (c * X + x)
    places = []
    for h in range(YL):
        for j in range(Z * YH):
            tile = turn ^ j
            tile = tile ^ ((tile & (X - 1)) >> 1)
            places.append((yl ^ c ^ h) * (CORE * X) + tile)
    grad_gram = grad_gram_of(
        rows_of,
        turned,
        jnp.stack(places + [yl]).astype(jnp.int32),
        yl,
        total,
    )

    return (input_gram, grad_gram)


def solution(mesh):
    placed = (P("tok", None), P("tok", None), P("tok", "tp"), P("tp", "tok"))
    return jax.shard_map(
        shards,
        mesh=mesh,
        in_specs=placed,
        out_specs=(P("tok", "tp"), P("tp", "tok")),
        check_vma=False,
    )
```

```python
import functools

import jax
import jax.numpy as jnp
from jax import lax
from jax.experimental import pallas as pl
from jax.experimental.pallas import tpu as pltpu
from jax.sharding import PartitionSpec as P

AXES = ("tok", "tp")
YL, X, CORE, Z, YH = 2, 4, 2, 4, 2
LANES = 128
LN2 = 0.6931471805599453
TINY = 1e-30


def contract_rows(left, right):
    return lax.dot_general(
        left, right, (((0,), (0,)), ((), ())), preferred_element_type=jnp.float32
    )


def contract_cols(left, right):
    return lax.dot_general(
        left, right, (((1,), (1,)), ((), ())), preferred_element_type=jnp.float32
    )


def index_of(yl, x, c, z, yh):
    return ((yl * X + x) * CORE + c) * (Z * YH) + z * YH + yh


def send(value, move):
    pairs = [
        (index_of(yl, x, c, z, yh), index_of(*move(yl, x, c, z, yh)))
        for yl in range(YL)
        for x in range(X)
        for c in range(CORE)
        for z in range(Z)
        for yh in range(YH)
    ]
    return lax.ppermute(value, AXES, pairs)


def over_core(value):
    return send(value, lambda yl, x, c, z, yh: (yl, x, 1 - c, z, yh))


def over_yl(value):
    return send(value, lambda yl, x, c, z, yh: (1 - yl, x, c, z, yh))


def over_other_y(value):
    return send(value, lambda yl, x, c, z, yh: (1 - yl, x, c, z, 1 - yh))


def over_yh(value):
    return send(value, lambda yl, x, c, z, yh: (yl, x, c, z, 1 - yh))


def over_x(value, k):
    return send(value, lambda yl, x, c, z, yh: (yl, x ^ k, c, z, yh))


def over_z(value, k):
    return send(value, lambda yl, x, c, z, yh: (yl, x, c, z ^ k, yh))


def turn_tp(yl, x, c, z, yh):
    p = (z * YH + yh) ^ (c * X + x)
    return yl, x, c, p // YH, p % YH


def turn_tok(yl, x, c, z, yh):
    s = (z * YH + yh) ^ (c * X + x)
    return s // X, s % X, yl, z, yh


def turn_tok_yh(yl, x, c, z, yh):
    yl, x, c, z, yh = turn_tok(yl, x, c, z, yh)
    return yl, x, c, z, 1 - yh


def part(value, index, count, axis):
    size = value.shape[axis] // count
    return lax.dynamic_slice_in_dim(value, index * size, size, axis)


def after(value, *others):
    return lax.optimization_barrier((value, *others))[0]


def scaled_kernel(contract, count, *refs):
    fields, weights, out_ref = refs[:count], refs[count:-1], refs[-1]
    size = weights[0].shape[1 if contract else 0]
    units = out_ref.shape[1] - LANES
    tile = 256
    blocks = [(field, i * size) for field in fields for i in range(field.shape[1] // size)]

    def step(n, top):
        columns = pl.ds(pl.multiple_of(n * tile, tile), tile)
        total = None
        for (field, start), weight in zip(blocks, weights):
            block = weight[columns, :] if contract else weight[:, columns]
            term = lax.dot_general(
                field[:, start : start + size],
                block,
                (((1,), (1 if contract else 0,)), ((), ())),
                preferred_element_type=jnp.float32,
            )
            total = term if total is None else total + term
        out_ref[:, columns] = total
        for i in range(tile // LANES):
            top = jnp.maximum(top, jnp.abs(total[:, i * LANES : (i + 1) * LANES]))
        return top

    top = lax.fori_loop(
        0, units // tile, step, jnp.zeros((out_ref.shape[0], LANES), jnp.float32)
    )
    top = jnp.maximum(jnp.max(top, axis=1, keepdims=True), TINY)
    exponent = jnp.floor(14.0 - jnp.log(top) / LN2)
    out_ref[:, :units] *= jnp.exp(exponent * LN2)
    out_ref[:, units:] = jnp.broadcast_to(exponent, (out_ref.shape[0], LANES))


def scaled_product(fields, weights, contract):
    units = weights[0].shape[0 if contract else 1]
    rows = fields[0].shape[0]
    depth = sum(weight.shape[1 if contract else 0] for weight in weights)
    vmem = pl.BlockSpec(memory_space=pltpu.VMEM)
    return pl.pallas_call(
        functools.partial(scaled_kernel, contract, len(fields)),
        out_shape=jax.ShapeDtypeStruct((rows, units + LANES), jnp.float32),
        in_specs=[vmem] * (len(fields) + len(weights)),
        out_specs=vmem,
        compiler_params=pltpu.CompilerParams(vmem_limit_bytes=16 * 2**20),
        cost_estimate=pl.CostEstimate(
            flops=2 * rows * depth * units,
            bytes_accessed=2 * depth * (rows + units) + 4 * rows * units,
            transcendentals=0,
        ),
        name="scaled_product",
    )(*fields, *weights)


def product_kernel(scale, left_ref, right_ref, out_ref):
    out_ref[...] = contract_rows(left_ref[...], right_ref[...]) * scale


def input_gram_of(left, right):
    total, rows = left.shape
    width = right.shape[1]
    tile = 256
    return pl.pallas_call(
        functools.partial(product_kernel, 1.0 / total),
        out_shape=jax.ShapeDtypeStruct((rows, width), jnp.float32),
        grid=(rows // tile,),
        in_specs=[
            pl.BlockSpec((total, tile), lambda n: (0, n)),
            pl.BlockSpec((total, width), lambda n: (0, 0)),
        ],
        out_specs=pl.BlockSpec((tile, width), lambda n: (n, 0)),
        compiler_params=pltpu.CompilerParams(vmem_limit_bytes=20 * 2**20),
        cost_estimate=pl.CostEstimate(
            flops=2 * total * rows * width,
            bytes_accessed=2 * total * (rows + width) + 4 * rows * width,
            transcendentals=0,
        ),
        name="input_gram",
    )(left, right)


def gram_kernel(scale, lefts, places, *refs):
    lefts, pieces = refs[:lefts], refs[lefts:-3]
    out_ref, right, sems = refs[-3:]
    b = pl.program_id(0)

    @pl.when((b == 0) & (pl.program_id(1) == 0))
    def _():
        copies = []
        tiles = [piece.at[j] for piece in pieces for j in range(piece.shape[0])]
        for i, tile in enumerate(tiles):
            for h in range(YL):
                slot = h * len(tiles) + i
                copies.append(
                    pltpu.make_async_copy(tile.at[h], right.at[places[slot]], sems.at[slot])
                )
        for copy in copies:
            copy.start()
        for copy in copies:
            copy.wait()

    def tokens(left, h):
        block = left[:, 0, h]
        return block.reshape(block.shape[0] * block.shape[1], block.shape[2])

    for which in range(YL):

        @pl.when(b == which)
        def _():
            block = jnp.concatenate(
                [tokens(left, h ^ which) for h in range(YL) for left in lefts], 0
            )
            rows = right[...]
            rows = rows.reshape(rows.shape[0] * rows.shape[1], rows.shape[2])
            out_ref[...] = contract_rows(block, rows) * scale


def grad_gram_of(lefts, pieces, places, yl, total):
    rows, units = lefts[0].shape[3:]
    tile = 512
    tiles = units // tile
    slots = YL * CORE * X
    return pl.pallas_call(
        functools.partial(gram_kernel, 1.0 / total, len(lefts)),
        out_shape=jax.ShapeDtypeStruct((YL * units, units), jnp.float32),
        grid_spec=pltpu.PrefetchScalarGridSpec(
            num_scalar_prefetch=1,
            grid=(YL, tiles),
            in_specs=[
                pl.BlockSpec(
                    (left.shape[0], 1, YL, rows, tile), lambda b, n, *_: (0, b, 0, 0, n)
                )
                for left in lefts
            ]
            + [pl.BlockSpec(memory_space=pltpu.HBM)] * len(pieces),
            out_specs=pl.BlockSpec(
                (tile, units), lambda b, n, places: ((places[slots] ^ b) * tiles + n, 0)
            ),
            scratch_shapes=[
                pltpu.VMEM((slots, rows, units), jnp.bfloat16),
                pltpu.SemaphoreType.DMA((slots,)),
            ],
        ),
        compiler_params=pltpu.CompilerParams(vmem_limit_bytes=58 * 2**20),
        cost_estimate=pl.CostEstimate(
            flops=2 * total * YL * units * units,
            bytes_accessed=6 * total * units + 8 * units * units,
            transcendentals=0,
        ),
        name="grad_gram",
    )(places, *lefts, *pieces)


def shards(layer_input, output_grad, gate_weight, down_weight):
    rows, model = layer_input.shape
    total = rows * YL * X * CORE
    place, band = lax.axis_index("tok"), lax.axis_index("tp")
    chip, c = place // CORE, place % CORE
    yl, x = chip // X, chip % X
    width = model // (YL * X)
    half = width // CORE

    def cut(field, *more):
        return [
            jnp.concatenate(
                [
                    part(field, (((yl ^ b) * X + (x ^ k)) * CORE + (c ^ d)), YL * X * CORE, 1)
                    for d in range(CORE)
                    for b in range(YL)
                ]
                + list(more),
                1,
            )
            for k in range(X)
        ]

    def swapped(pieces):
        return [pieces[1], pieces[0], pieces[3], pieces[2]]

    def halved(gate_part, hidden_part):
        lane = lax.broadcasted_iota(jnp.int32, (gate_part.shape[0], LANES), 1)
        exponents = jnp.where(
            lane < LANES // 2, gate_part[:, -LANES:], hidden_part[:, -LANES:]
        )
        parts = [gate_part[:, :-LANES], hidden_part[:, :-LANES], exponents]
        return jnp.concatenate(
            [part.astype(jnp.float16).reshape(X, rows, -1) for part in parts], 2
        )

    def exchanged(parts):
        return [parts[0]] + [over_x(parts[k], k) for k in range(1, X)]

    def summed(pieces, which):
        units = (pieces[0].shape[1] - LANES) // 2
        place = 2 * units + which * (LANES // 2)
        total_sum = None
        for piece in pieces:
            values = piece[:, which * units : (which + 1) * units].astype(jnp.float32)
            exponent = piece[:, place : place + 1].astype(jnp.float32)
            term = values * jnp.exp(exponent * -LN2)
            total_sum = term if total_sum is None else total_sum + term
        return total_sum

    def activated(gate, hidden):
        return (hidden * (gate / (1.0 + jnp.exp(-gate)))).astype(jnp.bfloat16)

    input_cut = cut(layer_input)
    gate_weight = after(gate_weight, *input_cut)
    gate_near = part(gate_weight, yl, YL, 1)
    gate_far = part(gate_weight, 1 - yl, YL, 1)
    gate_across = over_yl(gate_far)
    input_first = over_other_y(input_cut[0])
    pieces = [over_x(input_cut[k], k) for k in range(1, X)]
    own_band = part(layer_input, band, YL * X, 1)
    grad_cut = cut(output_grad, own_band)
    down_near, down_far = part(down_weight, yl, YL, 0), part(down_weight, 1 - yl, YL, 0)
    gate_across, input_first, pieces, grad_cut, down_far = lax.optimization_barrier(
        (gate_across, input_first, pieces, grad_cut, down_far)
    )
    gate_other = over_core(jnp.stack([gate_near, gate_across]))
    input_rest = over_other_y(jnp.concatenate(pieces, 0))
    down_across = over_yl(down_far)
    input_own = jnp.concatenate([input_cut[0]] + pieces, 0)
    grad_pieces = [over_x(grad_cut[k], k) for k in range(1, X)]

    gate_pieces = [gate_near, gate_across, gate_other[0], gate_other[1]]
    gate_part = scaled_product([input_own], gate_pieces, False)
    grad_pieces, down_across, input_rest, gate_part = lax.optimization_barrier(
        (grad_pieces, down_across, input_rest, gate_part)
    )
    down_other = over_core(jnp.stack([down_near, down_across]))
    down_pieces = [down_near, down_across, down_other[0], down_other[1]]
    grad_both = jnp.concatenate([grad_cut[0]] + grad_pieces, 0)
    far, near, band_own = jnp.split(grad_both, [width, 2 * width], 1)
    near, far, band_own, grad_both = lax.optimization_barrier((near, far, band_own, grad_both))
    near = over_yl(near)
    far = over_other_y(far)
    hidden_part = scaled_product([grad_both], down_pieces, True)
    first_sent = exchanged(halved(gate_part, hidden_part))
    input_other = jnp.concatenate([input_first, input_rest], 0)
    gate_part = scaled_product(
        [after(input_other, hidden_part)], swapped(gate_pieces), False
    )
    near, far = after([near, far], gate_part, first_sent[1], first_sent[3])
    hidden_part = scaled_product([far, near], swapped(down_pieces), True)
    second_sent = exchanged(halved(gate_part, hidden_part))
    band_other = over_yl(after(band_own, near))
    second_sent, band_other = lax.optimization_barrier((second_sent, band_other))

    def up_grads(sent):
        return activated(summed(sent, 0), summed(sent, 1))

    first = up_grads(after(first_sent, hidden_part))
    up_grad = jnp.stack([first, up_grads(after(second_sent, first))])
    moved = send(up_grad, turn_tp)
    both = jnp.stack([up_grad, over_yl(up_grad)])
    pair = jnp.stack([send(moved, turn_tok), send(moved, turn_tok_yh)])
    bands = jnp.stack([band_own, band_other])
    mine = jnp.stack([input_own[:, :half], input_other[:, half : 2 * half]])
    theirs = jnp.stack([input_own[:, 2 * half : 3 * half], input_other[:, 3 * half :]])
    across = over_core(after(jnp.concatenate([theirs, bands], 2), moved))
    pair, both, across = lax.optimization_barrier((pair, both, across))
    left = jnp.stack([mine, across[:, :, :half]]).reshape(total, half)
    right = jnp.stack([bands, across[:, :, half:]]).reshape(total, width)
    input_gram = input_gram_of(left, right)

    ring = [over_x(both, 1), over_x(both, 3), over_z(pair, 1), over_z(pair, 3)]
    ring, both, pair, input_gram = lax.optimization_barrier((ring, both, pair, input_gram))
    near_most = jnp.stack([both] + ring[:2])
    far_most = over_core(near_most)
    opposite = [
        over_x(ring[0][0], 3),
        over_x(ring[1][1], 1),
        over_z(ring[2][0], 3),
        over_z(ring[3][1], 1),
    ]
    opposite = lax.optimization_barrier(opposite)
    near_last = jnp.stack(opposite[:2])[None]
    turned = [pair, ring[2], opposite[2][None], opposite[3][None], ring[3]]
    rows_of = [near_most, near_last, far_most, over_core(near_last)]

    turn = band ^ chip ^ (c * X + x)
    places = []
    for h in range(YL):
        for j in range(Z * YH):
            tile = turn ^ j
            tile = tile ^ ((tile & (X - 1)) >> 1)
            places.append((yl ^ c ^ h) * (CORE * X) + tile)
    grad_gram = grad_gram_of(
        rows_of,
        turned,
        jnp.stack(places + [yl]).astype(jnp.int32),
        yl,
        total,
    )

    return (input_gram, grad_gram)


def solution(mesh):
    placed = (P("tok", None), P("tok", None), P("tok", "tp"), P("tp", "tok"))
    return jax.shard_map(
        shards,
        mesh=mesh,
        in_specs=placed,
        out_specs=(P("tok", "tp"), P("tp", "tok")),
        check_vma=False,
    )
```
